32 devices in a mesh: groups: 2 (over y), expert: 4 (over z), dp: 2 (over x), pair: 2 (over core).
Axes of the slice: x: 2, y: 2, z: 4, core: 2. Of those that a mesh axis runs over, the one named last changes fastest.
Arguments:
- out_grad: bfloat16 [4, 128, 4096], P(('groups', 'dp'), ('expert', 'pair')), parts along dimension 0, may hold values from -6 to 6
- merged: bfloat16 [4, 128, 4096], P(('groups', 'dp'), None, ('expert', 'pair')), parts along dimension 0, may hold values from -6 to 6
- sub_tokens: bfloat16 [4, 128, 4, 1024], P(('groups', 'dp'), ('expert', 'pair')), parts along dimension 0, may hold values from -6 to 6
- routes: int32 [4, 128, 4, 2], P(('groups', 'dp'), ('expert', 'pair')), parts along dimension 0, may hold values from 0 to 7, all different within a row; in each aligned block of 64 rows (0 to 63, 64 to 127, ..., all dimensions but the last counted through in order) at most 24 rows name the same one
- gate_probs: bfloat16 [4, 128, 4, 2], P(('groups', 'dp'), ('expert', 'pair')), parts along dimension 0, may hold values from 0.049804688 to 1
- merge_weight: bfloat16 [4096, 4096], P(('expert', 'pair'), 'dp'), may hold values from -0.09375 to 0.09375
- expert_in: bfloat16 [8, 1024, 1024], P(('expert', 'dp'), None, 'pair'), may hold values from -0.1875 to 0.1875
- expert_out: bfloat16 [8, 1024, 1024], P(('expert', 'dp'), 'pair'), may hold values from -0.1875 to 0.1875
Outputs:
- merge_grad: bfloat16 [8192, 4096], P(('groups', 'expert', 'pair'), 'dp'), parts along dimension 0
- grad_sub: bfloat16 [4, 128, 4, 1024], P(('groups', 'dp'), ('expert', 'pair')), parts along dimension 0
- grad_probs: bfloat16 [4, 128, 4, 2], P(('groups', 'dp'), ('expert', 'pair')), parts along dimension 0
- grad_in: bfloat16 [16, 1024, 1024], P(('groups', 'expert', 'dp'), None, 'pair'), parts along dimension 0
- grad_out: bfloat16 [16, 1024, 1024], P(('groups', 'expert', 'dp'), 'pair'), parts along dimension 0
The draws below stay inside these ranges and needn't reach their ends.
There are 2 independent parts, one for each index of `groups`. The reference program is written for one: setup_inputs(seed, part) draws one part's arguments, and reference() takes and returns one part's arrays. A program takes and returns all parts, laid end to end along the dimension named above; an argument that names none is the same for every part. Nothing has to cross between parts.
Inputs may be any that keep to these rules, and one draw needn't show every extreme that they name: `routes`: each sub-token names 2 different experts; the sub-tokens of one device name one expert at most 24 times.
All inputs are finite; a program needn't handle non-finite values.
Results may differ from the reference program's by a relative error of at most 0.0072.
Values may be sent and summed in bfloat16 or wider, within the bound.
A program may use at most 64 MiB of HBM per device.

```python
import math
import jax
import jax.numpy as jnp
import numpy as np
from jax import lax

D = 4096
HEADS = 4
HID = 1024
TOPK = 2
POS_DEV = 16
DH = 1024
HALF = 512
EXPERTS = 8
SEQS = 2
LEN = 128
CAP = 24
N_EXPERT = 4
N_DP = 2
N_PAIR = 2


def levels(stream_key, dims, pieces, low, high):
    gain, own = 1.0, jax.random.fold_in(stream_key, 6)
    for dim, shards_of in pieces:
        heights = jnp.exp(jax.random.uniform(jax.random.fold_in(own, dim), (shards_of,), jnp.float32, low / len(pieces), high / len(pieces)))
        gain = gain * jnp.repeat(heights, dims[dim] // shards_of).reshape([-1 if axis == dim else 1 for axis in range(len(dims))])
    return gain


def assign_block(own_key, own, number, rows, number_of, top, most, skew):
    order = jax.random.permutation(own_key, number_of)
    crowded, usual = portions_of(number_of, rows * top, most, skew, True), portions_of(number_of, rows * top, most, skew, False)
    places = jnp.arange(number_of)

    def named(tallies, turn):
        used = int((tallies > 0).sum())
        fixed = max(1, used // 4)
        shifted = fixed + (places - fixed + turn * (used - fixed)) % max(1, number_of - fixed)
        return jnp.zeros((number_of,), jnp.int32).at[order[jnp.where(places < fixed, places, shifted)]].set(jnp.asarray(tallies, jnp.int32))

    tallies = jnp.where(number % 4 == 0, named(crowded, number // 4), named(usual, number - number // 4 - 1))
    mixed = jax.random.permutation(jax.random.fold_in(own, 3), number_of)
    giver, sink = mixed[0:number_of // 2 * 2:2], mixed[1:number_of // 2 * 2:2]
    margin = jnp.minimum(tallies[giver] - 1, most - tallies[sink]) // 2
    margin = jnp.where((giver == order[0]) | (sink == order[0]) | (tallies[sink] == 0), 0, jnp.maximum(margin, 0))
    shifted = jax.random.randint(jax.random.fold_in(own, 4), (number_of // 2,), 0, 1 << 20) % (margin + 1)
    tallies = tallies.at[giver].add(-shifted).at[sink].add(shifted)
    labels = jnp.searchsorted(jnp.cumsum(tallies), jnp.arange(rows * top), side="right").astype(jnp.int32)
    table = labels.reshape(top, rows).T
    table = table[jax.random.permutation(jax.random.fold_in(own, 1), rows)]
    turn = jax.random.randint(jax.random.fold_in(own, 2), (rows, 1), 0, top)
    return jnp.take_along_axis(table, (jnp.arange(top)[None, :] + turn) % top, axis=1)


def portions_of(number_of, total, most, lean, full):
    weights = [(1 << 20) // math.isqrt(rank ** lean) + 1 for rank in range(1, number_of + 1)]
    largest = most if full else min(most, max(-(-total // number_of), total * weights[0] // sum(weights)))
    least = 1 if total - largest >= number_of - 1 else 0
    counts, rest = [largest] + [least] * (number_of - 1), total - largest - least * (number_of - 1)
    while rest > 0:
        free = [i for i in range(1, number_of) if counts[i] < largest] or [i for i in range(1, number_of) if counts[i] < most]
        whole, left = sum([weights[i] for i in free]), rest
        for i in free:
            extra = min(most - counts[i], max(1, left * weights[i] // whole), rest)
            counts[i] = counts[i] + extra
            rest = rest - extra
    return np.array(counts)


def noise(stream_key, shape, spread, limit, cuts=(), held_as=jnp.bfloat16):
    factor_of = levels(stream_key, shape, cuts, -0.22, 0.18) if cuts else 1.0
    result = jax.random.normal(stream_key, shape, jnp.float32) * spread * factor_of
    return jnp.minimum(jnp.maximum(result, -limit), limit).astype(held_as)


def setup_inputs(seed: int = 0, part: int = 0) -> dict:
    key_of = jax.random.split(jax.random.key(seed), 9)
    own_keys = jax.random.split(jax.random.fold_in(key_of[8], part), 9)
    out_grad = noise(own_keys[0], (SEQS, LEN, D), 1.0, 6.0, ((0, 2), (1, 8)))
    merged = noise(own_keys[1], (SEQS, LEN, D), 1.0, 6.0, ((0, 2), (2, 8)))
    sub_tokens = noise(own_keys[2], (SEQS, LEN, HEADS, DH), 1.0, 6.0, ((0, 2), (1, 8)))
    routes_keys = jax.random.split(jax.random.fold_in(own_keys[3], 1), SEQS * LEN * HEADS // (POS_DEV * HEADS))
    routes_turns = jax.random.permutation(jax.random.fold_in(own_keys[3], 3), SEQS * LEN * HEADS // (POS_DEV * HEADS))
    routes = jax.vmap(lambda own, number: assign_block(jax.random.fold_in(own_keys[3], 2), own, number, POS_DEV * HEADS, EXPERTS, TOPK, CAP, 2))(routes_keys, routes_turns).reshape((SEQS, LEN, HEADS, TOPK))
    gate_probs = jnp.clip(jnp.exp(math.log(1.0) - 2.9996462 * jax.random.uniform(own_keys[4], (SEQS, LEN, HEADS, TOPK), jnp.float32) ** levels(own_keys[4], (SEQS, LEN, HEADS, TOPK), ((0, 2), (1, 8)), -0.2, 0.2)), 0.049804688, 1.0).astype(jnp.bfloat16)
    merge_weight = noise(key_of[5], (D, D), D ** -0.5, 0.09375, ((0, 8), (1, 2)))
    expert_in = noise(key_of[6], (EXPERTS, DH, HID), DH ** -0.5, 0.1875, ((0, 8), (2, 2)))
    expert_out = noise(key_of[7], (EXPERTS, HID, DH), HID ** -0.5, 0.1875, ((0, 8), (1, 2)))
    return {"out_grad": out_grad, "merged": merged, "sub_tokens": sub_tokens, "routes": routes, "gate_probs": gate_probs, "merge_weight": merge_weight, "expert_in": expert_in, "expert_out": expert_out}


def expert_block(inputs, head_part, gates, first, second):
    preact = jnp.dot(inputs, first, preferred_element_type=jnp.float32)
    activated, pullback = jax.vjp(jax.nn.gelu, preact)
    back_hidden = jnp.dot(head_part, second.T, preferred_element_type=jnp.float32)
    prob_half = lax.optimization_barrier(jnp.sum(activated * back_hidden, axis=1))
    scales = gates.astype(jnp.float32)[:, None]
    hidden_grad = pullback(scales * back_hidden)[0].astype(jnp.bfloat16)
    out_scaled = (scales * head_part.astype(jnp.float32)).astype(jnp.bfloat16)
    act_low = activated.astype(jnp.bfloat16)
    grad_first = jnp.dot(inputs.T, hidden_grad, preferred_element_type=jnp.float32)
    grad_second = jnp.dot(act_low.T, out_scaled, preferred_element_type=jnp.float32)
    input_half = jnp.dot(hidden_grad, first.T, preferred_element_type=jnp.float32)
    return (input_half, prob_half, grad_first, grad_second)

def rounded(value):
    return lax.optimization_barrier(value.astype(jnp.bfloat16)).astype(jnp.float32)

def reference(out_grad, merged, sub_tokens, routes, gate_probs, merge_weight, expert_in, expert_out):
    token_count = SEQS * LEN
    flat_grad = out_grad.reshape(token_count, D)
    head_grad = jnp.dot(flat_grad, merge_weight.T, preferred_element_type=jnp.float32).astype(jnp.bfloat16)
    merge_grad = jnp.dot(merged.reshape(token_count, D).T, flat_grad, preferred_element_type=jnp.float32).astype(jnp.bfloat16)
    sub_count = token_count * HEADS
    inputs_all = sub_tokens.reshape(sub_count, DH)
    heads_all = head_grad.reshape(sub_count, DH)
    routed = routes.reshape(sub_count * TOPK).astype(jnp.int32)
    gates_all = gate_probs.reshape(sub_count * TOPK)
    order = jnp.argsort(routed, stable=True).astype(jnp.int32)
    loads = lax.optimization_barrier(jnp.sum((routed[:, None] == jnp.arange(EXPERTS, dtype=jnp.int32)[None, :]).astype(jnp.int32), axis=0))
    starts = (jnp.cumsum(loads) - loads).astype(jnp.int32)
    most_rows = N_EXPERT * N_DP * N_PAIR * CAP
    order_pad = jnp.concatenate([order, jnp.zeros((most_rows,), jnp.int32)])

    def per_expert(carry, packed):
        input_acc, prob_acc = carry
        first_w, second_w, start, load = packed
        picked = lax.dynamic_slice_in_dim(order_pad, start.astype(jnp.int32), most_rows)
        valid = jnp.arange(most_rows, dtype=jnp.int32) < load
        owner = (picked // TOPK).astype(jnp.int32)
        inputs = jnp.where(valid[:, None], inputs_all[owner], jnp.zeros((), jnp.bfloat16))
        head_part = jnp.where(valid[:, None], heads_all[owner], jnp.zeros((), jnp.bfloat16))
        gates = jnp.where(valid, gates_all[picked], jnp.zeros((), jnp.bfloat16))
        input_sum = jnp.zeros((most_rows, DH), jnp.float32)
        prob_sum = jnp.zeros((most_rows,), jnp.float32)
        firsts = []
        seconds = []
        for half in range(HID // HALF):
            input_half, prob_half, grad_first, grad_second = expert_block(inputs, head_part, gates, first_w[:, half * HALF:(half + 1) * HALF], second_w[half * HALF:(half + 1) * HALF, :])
            input_sum = input_sum + rounded(input_half)
            prob_sum = prob_sum + rounded(prob_half)
            firsts.append(grad_first)
            seconds.append(grad_second)
        input_acc = input_acc.at[owner].add(jnp.where(valid[:, None], rounded(input_sum), jnp.zeros((), jnp.float32)))
        prob_acc = prob_acc.at[picked].add(jnp.where(valid, rounded(prob_sum), jnp.zeros((), jnp.float32)))
        grad_in_one = jnp.concatenate(firsts, axis=1).astype(jnp.bfloat16)
        grad_out_one = jnp.concatenate(seconds, axis=0).astype(jnp.bfloat16)
        return ((input_acc, prob_acc), (grad_in_one, grad_out_one))
    initial = (jnp.zeros((sub_count, DH), jnp.float32), jnp.zeros((sub_count * TOPK,), jnp.float32))
    (input_acc, prob_acc), (grad_in, grad_out) = lax.scan(per_expert, initial, (expert_in, expert_out, starts, loads))
    grad_sub = input_acc.astype(jnp.bfloat16).reshape(SEQS, LEN, HEADS, DH)
    grad_probs = prob_acc.astype(jnp.bfloat16).reshape(SEQS, LEN, HEADS, TOPK)
    return (merge_grad, grad_sub, grad_probs, grad_in, grad_out)
```

```python
import jax
import jax.numpy as jnp
from jax import lax
from jax.sharding import PartitionSpec as P


def expert_block(inputs, head_part, gates, first, second):
    preact = jnp.dot(inputs, first, preferred_element_type=jnp.float32)
    activated, pullback = jax.vjp(jax.nn.gelu, preact)
    back_hidden = lax.dot_general(
        head_part, second, (((1,), (1,)), ((), ())), preferred_element_type=jnp.float32
    )
    prob_half = jnp.sum(activated * back_hidden, axis=1)
    scales = gates.astype(jnp.float32)[:, None]
    hidden_grad = pullback(scales * back_hidden)[0].astype(jnp.bfloat16)
    out_scaled = (scales * head_part.astype(jnp.float32)).astype(jnp.bfloat16)
    act_low = activated.astype(jnp.bfloat16)
    grad_first = lax.dot_general(
        inputs, hidden_grad, (((0,), (0,)), ((), ())), preferred_element_type=jnp.float32
    )
    grad_second = lax.dot_general(
        act_low, out_scaled, (((0,), (0,)), ((), ())), preferred_element_type=jnp.float32
    )
    input_half = lax.dot_general(
        hidden_grad, first, (((1,), (1,)), ((), ())), preferred_element_type=jnp.float32
    )
    return (input_half, prob_half, grad_first, grad_second)


def slots_of(routes, experts, capacity):
    flat = routes.reshape(-1)
    top = routes.shape[-1]
    onehot = (flat[:, None] == jnp.arange(experts, dtype=jnp.int32)[None, :]).astype(jnp.int32)
    rank = jnp.sum((jnp.cumsum(onehot, axis=0) - onehot) * onehot, axis=1)
    return (flat * capacity + rank).reshape(-1, top)


def per_device(
    out_grad, merged, sub_tokens, routes, gate_probs, merge_weight, expert_in, expert_out
):
    experts = lax.axis_size("expert") * lax.axis_size("dp")
    data_size = lax.axis_size("dp")
    length, feats = merged.shape[1:]
    positions, head_count, head_dim = sub_tokens.shape[1:]
    top_count = routes.shape[3]
    subs = positions * head_count
    routed_count = subs * top_count
    capacity = max(2, 3 * routed_count // (2 * experts))
    slot_count = experts * capacity
    columns = lax.all_to_all(out_grad[0], "dp", split_axis=1, concat_axis=0, tiled=True)
    width = columns.shape[1]
    tokens = lax.all_gather(columns, ("expert", "pair"), axis=0, tiled=False)
    tokens = tokens.reshape(-1, data_size, positions, width).transpose(1, 0, 2, 3)
    tokens = tokens.reshape(data_size * length, width)
    saved = lax.all_gather(merged[0], "dp", axis=0, tiled=True)
    partial = lax.dot_general(
        tokens, merge_weight, (((1,), (1,)), ((), ())), preferred_element_type=jnp.float32
    ).reshape(data_size, length, feats)
    partial = lax.all_to_all(partial, "dp", split_axis=0, concat_axis=0, tiled=True)
    head_block = jnp.sum(partial, axis=0).astype(jnp.bfloat16)
    head_grad = lax.all_to_all(
        head_block, ("expert", "pair"), split_axis=0, concat_axis=1, tiled=True
    ).reshape(subs, head_dim)
    merge_grad = lax.dot_general(
        saved, tokens, (((0,), (0,)), ((), ())), preferred_element_type=jnp.float32
    ).astype(jnp.bfloat16)

    slots = slots_of(routes[0], experts, capacity)
    numbers = jnp.arange(slot_count, dtype=jnp.int32)
    hits = (slots[None, :, :] == numbers[:, None, None]).astype(jnp.bfloat16)
    pick = jnp.sum(hits, axis=2)
    gates = jnp.sum(
        hits.astype(jnp.float32)
        * gate_probs[0].reshape(1, subs, top_count).astype(jnp.float32),
        axis=(1, 2),
    ).astype(jnp.bfloat16)
    extra = jnp.broadcast_to(gates[:, None], (slot_count, 128))

    def select(rows):
        return jnp.dot(pick, rows, preferred_element_type=jnp.float32).astype(jnp.bfloat16)

    send_inputs = jnp.concatenate(
        [select(sub_tokens[0].reshape(subs, head_dim)), extra], axis=1
    ).reshape(experts, capacity, head_dim + 128)
    send_heads = select(head_grad).reshape(experts, capacity, head_dim)

    def spread(rows):
        got = lax.all_to_all(rows, ("expert", "dp"), split_axis=0, concat_axis=0, tiled=True)
        return lax.all_gather(got, "pair", axis=0, tiled=True).reshape(-1, rows.shape[2])

    inputs = spread(send_inputs)
    heads = spread(send_heads)
    first = expert_in[0]
    second = expert_out[0]
    input_part, prob_part, grads_first, grads_second = expert_block(
        inputs[:, :head_dim], heads, inputs[:, head_dim], first, second
    )
    both = jnp.concatenate(
        [input_part, jnp.broadcast_to(prob_part[:, None], (prob_part.shape[0], 128))], axis=1
    ).astype(jnp.bfloat16)
    summed = lax.psum_scatter(
        both.reshape(2 * experts, capacity, head_dim + 128),
        "pair",
        scatter_dimension=0,
        tiled=True,
    )
    back = lax.all_to_all(summed, ("expert", "dp"), split_axis=0, concat_axis=0, tiled=True)
    back = back.reshape(slot_count, head_dim + 128)
    grad_sub = lax.dot_general(
        pick, back[:, :head_dim], (((0,), (0,)), ((), ())), preferred_element_type=jnp.float32
    ).astype(jnp.bfloat16)
    grad_probs = jnp.sum(
        hits.astype(jnp.float32) * back[:, head_dim].astype(jnp.float32)[:, None, None], axis=0
    ).astype(jnp.bfloat16)
    return (
        merge_grad,
        grad_sub.reshape(sub_tokens.shape),
        grad_probs.reshape(gate_probs.shape),
        grads_first.astype(jnp.bfloat16).reshape(expert_in.shape),
        grads_second.astype(jnp.bfloat16).reshape(expert_out.shape),
    )


def solution(mesh):
    placed = (
        P(("groups", "dp"), ("expert", "pair"), None),
        P(("groups", "dp"), None, ("expert", "pair")),
        P(("groups", "dp"), ("expert", "pair"), None, None),
        P(("groups", "dp"), ("expert", "pair"), None, None),
        P(("groups", "dp"), ("expert", "pair"), None, None),
        P(("expert", "pair"), "dp"),
        P(("expert", "dp"), None, "pair"),
        P(("expert", "dp"), "pair", None),
    )
    return jax.shard_map(
        per_device,
        mesh=mesh,
        in_specs=placed,
        out_specs=(
            P(("groups", "expert", "pair"), "dp"),
            P(("groups", "dp"), ("expert", "pair"), None, None),
            P(("groups", "dp"), ("expert", "pair"), None, None),
            P(("groups", "expert", "dp"), None, "pair"),
            P(("groups", "expert", "dp"), "pair", None),
        ),
        check_vma=False,
    )
```

```python
import functools

import jax
import jax.numpy as jnp
from jax import lax
from jax.experimental import pallas as pl
from jax.experimental.pallas import tpu as pltpu
from jax.sharding import PartitionSpec as P


def expert_block(inputs, head_part, gates, first, second):
    preact = jnp.dot(inputs, first, preferred_element_type=jnp.float32)
    activated, pullback = jax.vjp(jax.nn.gelu, preact)
    back_hidden = lax.dot_general(
        head_part, second, (((1,), (1,)), ((), ())), preferred_element_type=jnp.float32
    )
    prob_half = jnp.sum(activated * back_hidden, axis=1)
    scales = gates.astype(jnp.float32)[:, None]
    hidden_grad = pullback(scales * back_hidden)[0].astype(jnp.bfloat16)
    out_scaled = (scales * head_part.astype(jnp.float32)).astype(jnp.bfloat16)
    act_low = activated.astype(jnp.bfloat16)
    grad_first = lax.dot_general(
        inputs, hidden_grad, (((0,), (0,)), ((), ())), preferred_element_type=jnp.float32
    )
    grad_second = lax.dot_general(
        act_low, out_scaled, (((0,), (0,)), ((), ())), preferred_element_type=jnp.float32
    )
    input_half = lax.dot_general(
        hidden_grad, first, (((1,), (1,)), ((), ())), preferred_element_type=jnp.float32
    )
    return (input_half, prob_half, grad_first, grad_second)


def slots_of(routes, experts, capacity):
    flat = routes.reshape(-1)
    top = routes.shape[-1]
    onehot = (flat[:, None] == jnp.arange(experts, dtype=jnp.int32)[None, :]).astype(jnp.int32)
    rank = jnp.sum((jnp.cumsum(onehot, axis=0) - onehot) * onehot, axis=1)
    return (flat * capacity + rank).reshape(-1, top)


def spread_plan(
    out_grad, merged, sub_tokens, routes, gate_probs, merge_weight, expert_in, expert_out
):
    experts = lax.axis_size("expert") * lax.axis_size("dp")
    data_size = lax.axis_size("dp")
    length, feats = merged.shape[1:]
    positions, head_count, head_dim = sub_tokens.shape[1:]
    top_count = routes.shape[3]
    subs = positions * head_count
    routed_count = subs * top_count
    capacity = max(2, 3 * routed_count // (2 * experts))
    slot_count = experts * capacity
    columns = lax.all_to_all(out_grad[0], "dp", split_axis=1, concat_axis=0, tiled=True)
    width = columns.shape[1]
    tokens = lax.all_gather(columns, ("expert", "pair"), axis=0, tiled=False)
    tokens = tokens.reshape(-1, data_size, positions, width).transpose(1, 0, 2, 3)
    tokens = tokens.reshape(data_size * length, width)
    saved = lax.all_gather(merged[0], "dp", axis=0, tiled=True)
    partial = lax.dot_general(
        tokens, merge_weight, (((1,), (1,)), ((), ())), preferred_element_type=jnp.float32
    ).reshape(data_size, length, feats)
    partial = lax.all_to_all(partial, "dp", split_axis=0, concat_axis=0, tiled=True)
    head_block = jnp.sum(partial, axis=0).astype(jnp.bfloat16)
    head_grad = lax.all_to_all(
        head_block, ("expert", "pair"), split_axis=0, concat_axis=1, tiled=True
    ).reshape(subs, head_dim)
    merge_grad = lax.dot_general(
        saved, tokens, (((0,), (0,)), ((), ())), preferred_element_type=jnp.float32
    ).astype(jnp.bfloat16)

    slots = slots_of(routes[0], experts, capacity)
    numbers = jnp.arange(slot_count, dtype=jnp.int32)
    hits = (slots[None, :, :] == numbers[:, None, None]).astype(jnp.bfloat16)
    pick = jnp.sum(hits, axis=2)
    gates = jnp.sum(
        hits.astype(jnp.float32)
        * gate_probs[0].reshape(1, subs, top_count).astype(jnp.float32),
        axis=(1, 2),
    ).astype(jnp.bfloat16)
    extra = jnp.broadcast_to(gates[:, None], (slot_count, 128))

    def select(rows):
        return jnp.dot(pick, rows, preferred_element_type=jnp.float32).astype(jnp.bfloat16)

    send_inputs = jnp.concatenate(
        [select(sub_tokens[0].reshape(subs, head_dim)), extra], axis=1
    ).reshape(experts, capacity, head_dim + 128)
    send_heads = select(head_grad).reshape(experts, capacity, head_dim)

    def spread(rows):
        got = lax.all_to_all(rows, ("expert", "dp"), split_axis=0, concat_axis=0, tiled=True)
        return lax.all_gather(got, "pair", axis=0, tiled=True).reshape(-1, rows.shape[2])

    inputs = spread(send_inputs)
    heads = spread(send_heads)
    first = expert_in[0]
    second = expert_out[0]
    input_part, prob_part, grads_first, grads_second = expert_block(
        inputs[:, :head_dim], heads, inputs[:, head_dim], first, second
    )
    both = jnp.concatenate(
        [input_part, jnp.broadcast_to(prob_part[:, None], (prob_part.shape[0], 128))], axis=1
    ).astype(jnp.bfloat16)
    summed = lax.psum_scatter(
        both.reshape(2 * experts, capacity, head_dim + 128),
        "pair",
        scatter_dimension=0,
        tiled=True,
    )
    back = lax.all_to_all(summed, ("expert", "dp"), split_axis=0, concat_axis=0, tiled=True)
    back = back.reshape(slot_count, head_dim + 128)
    grad_sub = lax.dot_general(
        pick, back[:, :head_dim], (((0,), (0,)), ((), ())), preferred_element_type=jnp.float32
    ).astype(jnp.bfloat16)
    grad_probs = jnp.sum(
        hits.astype(jnp.float32) * back[:, head_dim].astype(jnp.float32)[:, None, None], axis=0
    ).astype(jnp.bfloat16)
    return (
        merge_grad,
        grad_sub.reshape(sub_tokens.shape),
        grad_probs.reshape(gate_probs.shape),
        grads_first.astype(jnp.bfloat16).reshape(expert_in.shape),
        grads_second.astype(jnp.bfloat16).reshape(expert_out.shape),
    )


MESH = pl.DeviceIdType.MESH
LANES = 128


def across(left, right, dims):
    return lax.dot_general(left, right, ((dims[0], dims[1]), ((), ())), preferred_element_type=jnp.float32)


def rows_of(value):
    return value.astype(jnp.float32).reshape(-1, value.shape[-1]).astype(jnp.bfloat16)


def layer_kernel(
    e_size, d_size, capacity, heads,
    ids_row, ids_col, gates_row, og, saved, subs, w_any, first_any, second_any,
    merge_any, sub_out, probs_out, in_any, out_any,
    w, first, second, merge_out, in_out, out_out,
    og_buf, saved_buf, send_u, recv_u, send_g, recv_g, part_buf, home_buf, half_buf, pair_buf,
    ret_buf, back_buf,
    load_sem, store_sem, og_s, og_r, ogf_s, ogf_r, sv_s, sv_r, u_s, u_r, uf_s, uf_r, g_s, g_r, gf_s, gf_r,
    pt_s, pt_r, hf_s, hf_r, rt_s, rt_r,
):
    e, d, p = lax.axis_index("expert"), lax.axis_index("dp"), lax.axis_index("pair")
    owners = e_size * d_size
    me = e * d_size + d
    other = 1 - p
    positions, wide = og.shape
    half_cols = wide // d_size
    feats = saved.shape[1]
    head_dim = wide // heads
    slot_count = owners * capacity
    count = ids_row.shape[1]
    sub_rows = count // 2

    def place(t, q):
        return {"expert": t // d_size, "dp": lax.rem(t, d_size), "pair": q}

    def remote(src, dst, send, recv, t, q):
        return pltpu.make_async_remote_copy(
            src_ref=src, dst_ref=dst, send_sem=send, recv_sem=recv,
            device_id=place(t, q), device_id_type=MESH,
        )

    loads = [
        pltpu.make_async_copy(w_any, w, load_sem.at[0]),
        pltpu.make_async_copy(first_any, first, load_sem.at[1]),
        pltpu.make_async_copy(second_any, second, load_sem.at[2]),
    ]
    for load in loads:
        load.start()

    barrier = pltpu.get_barrier_semaphore()
    mine = me * 2 + p
    for step in range(1, 2 * owners):
        q = lax.rem(mine + step, 2 * owners)
        pl.semaphore_signal(
            barrier, inc=1, device_id=place(q // 2, lax.rem(q, 2)), device_id_type=MESH
        )

    before = lax.broadcasted_iota(jnp.int32, (count, count), 0) < lax.broadcasted_iota(
        jnp.int32, (count, count), 1
    )
    same = ids_col[...] == ids_row[...]
    rank = jnp.sum(jnp.where(before & same, 1.0, 0.0), axis=0, keepdims=True).astype(jnp.int32)
    slots = ids_row[...] * capacity + rank
    hits = jnp.where(
        lax.broadcasted_iota(jnp.int32, (slot_count, count), 0) == slots, 1.0, 0.0
    )
    pick = (hits[:, :sub_rows] + hits[:, sub_rows:]).astype(jnp.bfloat16)
    gate = jnp.sum(hits * gates_row[...], axis=1, keepdims=True)
    stacked = jnp.concatenate(
        [subs[:, h * head_dim : (h + 1) * head_dim] for h in range(heads)], axis=0
    )
    send_u[:, :, :head_dim] = (
        across(pick, stacked, ((1,), (0,))).reshape(owners, capacity, head_dim).astype(jnp.bfloat16)
    )
    send_u[:, :, head_dim:] = (
        jnp.broadcast_to(gate, (slot_count, LANES))
        .reshape(owners, capacity, LANES)
        .astype(jnp.bfloat16)
    )
    pl.semaphore_wait(barrier, 2 * owners - 1)

    sends = []

    def go(copy):
        copy.start()
        sends.append(copy)

    def columns(t):
        return og.at[:, pl.ds(pl.multiple_of(lax.rem(t, d_size) * half_cols, LANES), half_cols)]

    for step in range(1, owners):
        t = lax.rem(me + step, owners)
        go(remote(columns(t), og_buf.at[p, me], og_s.at[step], og_r.at[me], t, p))
    go(remote(columns(me), og_buf.at[p, me], ogf_s.at[me], ogf_r.at[me], me, other))
    own_og = pltpu.make_async_copy(columns(me), og_buf.at[p, me], load_sem.at[3])
    own_og.start()
    for step in range(1, d_size):
        t = e * d_size + lax.rem(d + step, d_size)
        go(remote(saved, saved_buf.at[d], sv_s.at[step], sv_r.at[d], t, p))
    saved_buf[d] = saved[...]
    for step in range(1, owners):
        t = lax.rem(me + step, owners)
        go(remote(send_u.at[t], recv_u.at[p, me], u_s.at[step], u_r.at[me], t, p))
    go(remote(send_u.at[me], recv_u.at[p, me], uf_s.at[me], uf_r.at[me], me, other))
    recv_u[p, me] = send_u[me]

    def pass_on(buf, recv, fsend, frecv):
        for step in range(1, owners):
            t = lax.rem(me + owners - step, owners)
            remote(buf.at[p, t], buf.at[p, t], fsend.at[t], recv.at[t], me, other).wait_recv()
            go(remote(buf.at[p, t], buf.at[p, t], fsend.at[t], frecv.at[t], me, other))

    def from_pair(buf, fsend, frecv):
        for t in range(owners):
            remote(
                buf.at[other, t], buf.at[other, t], fsend.at[t], frecv.at[t], me, other
            ).wait_recv()

    pass_on(og_buf, og_r, ogf_s, ogf_r)
    own_og.wait()
    loads[0].wait()
    from_pair(og_buf, ogf_s, ogf_r)
    tokens = og_buf[...].reshape(2 * owners * positions, half_cols)
    part_buf[...] = (
        across(tokens, w[...], ((1,), (1,)))
        .astype(jnp.bfloat16)
        .reshape(2, owners, positions, feats)
    )
    for step in range(1, 2 * owners):
        q = lax.rem(mine + step, 2 * owners)
        t, qp = q // 2, lax.rem(q, 2)
        go(remote(part_buf.at[qp, t], home_buf.at[p, me], pt_s.at[step], pt_r.at[p, me], t, qp))
    home_buf[p, me] = part_buf[p, me]
    for step in range(1, 2 * owners):
        q = lax.rem(mine + 2 * owners - step, 2 * owners)
        t, qp = q // 2, lax.rem(q, 2)
        remote(
            home_buf.at[qp, t], home_buf.at[qp, t], pt_s.at[step], pt_r.at[qp, t], me, other
        ).wait_recv()
    blocks = []
    for i in range(e_size):
        for q in range(2):
            total = home_buf[q, i * d_size].astype(jnp.float32)
            for j in range(1, d_size):
                total = total + home_buf[q, i * d_size + j].astype(jnp.float32)
            blocks.append(total.astype(jnp.bfloat16))
    per_head = head_dim // feats
    head_rows = jnp.concatenate(
        [
            jnp.concatenate(blocks[h * per_head : (h + 1) * per_head], axis=1)
            for h in range(heads)
        ],
        axis=0,
    )
    send_g[...] = (
        across(pick, head_rows, ((1,), (0,)))
        .reshape(owners, capacity, head_dim)
        .astype(jnp.bfloat16)
    )
    for step in range(1, owners):
        t = lax.rem(me + step, owners)
        go(remote(send_g.at[t], recv_g.at[p, me], g_s.at[step], g_r.at[me], t, p))
    go(remote(send_g.at[me], recv_g.at[p, me], gf_s.at[me], gf_r.at[me], me, other))
    recv_g[p, me] = send_g[me]

    pass_on(recv_u, u_r, uf_s, uf_r)
    for step in range(1, d_size):
        j = lax.rem(d + step, d_size)
        remote(saved, saved_buf.at[j], sv_s.at[step], sv_r.at[j], me, other).wait_recv()
    ordered = jnp.concatenate(
        [
            saved_buf[j, (i * 2 + q) * positions : (i * 2 + q + 1) * positions, :]
            for q in range(2)
            for i in range(e_size)
            for j in range(d_size)
        ],
        axis=0,
    )
    merge_out[...] = across(ordered, tokens, ((0,), (0,))).astype(jnp.bfloat16)
    stores = [pltpu.make_async_copy(merge_out, merge_any, store_sem.at[0])]
    stores[0].start()
    from_pair(recv_u, uf_s, uf_r)
    inputs = rows_of(recv_u[:, :, :, :head_dim])
    scales = recv_u[:, :, :, head_dim:].astype(jnp.float32).reshape(-1, LANES)[:, :1]
    loads[1].wait()
    loads[2].wait()
    preact = across(inputs, first[...], ((1,), (0,)))
    root = 0.7978845608028654
    bend = jnp.tanh(root * (preact + 0.044715 * (preact * preact * preact)))
    activated = 0.5 * preact * (1.0 + bend)
    slope = 0.5 * (1.0 + bend) + 0.5 * preact * (1.0 - bend * bend) * (
        root * (1.0 + 3.0 * 0.044715 * (preact * preact))
    )

    pass_on(recv_g, g_r, gf_s, gf_r)
    from_pair(recv_g, gf_s, gf_r)
    grads = rows_of(recv_g[...])
    back = across(grads, second[...], ((1,), (1,)))
    hidden = (slope * (scales * back)).astype(jnp.bfloat16)
    half_buf[:, :, :, head_dim:] = (
        jnp.broadcast_to(
            jnp.sum(activated * back, axis=1, keepdims=True), (2 * slot_count, LANES)
        )
        .reshape(2, owners, capacity, LANES)
        .astype(jnp.bfloat16)
    )
    half_buf[:, :, :, :head_dim] = (
        across(hidden, first[...], ((1,), (1,)))
        .reshape(2, owners, capacity, head_dim)
        .astype(jnp.bfloat16)
    )
    order = [lax.rem(me + step, owners) for step in list(range(1, owners)) + [0]]
    for t in order:
        go(remote(half_buf.at[other, t], pair_buf.at[t], hf_s.at[t], hf_r.at[t], me, other))
    for step, t in enumerate(order):
        remote(half_buf.at[other, t], pair_buf.at[t], hf_s.at[t], hf_r.at[t], me, other).wait_recv()
        ret_buf[t] = (
            half_buf[p, t].astype(jnp.float32) + pair_buf[t].astype(jnp.float32)
        ).astype(jnp.bfloat16)
        if step < owners - 1:
            go(remote(ret_buf.at[t], back_buf.at[me], rt_s.at[step], rt_r.at[me], t, p))
    back_buf[me] = ret_buf[me]

    in_out[...] = across(inputs, hidden, ((0,), (0,))).astype(jnp.bfloat16)
    stores.append(pltpu.make_async_copy(in_out, in_any, store_sem.at[1]))
    stores[1].start()
    scaled = (scales * grads.astype(jnp.float32)).astype(jnp.bfloat16)
    out_out[...] = across(activated.astype(jnp.bfloat16), scaled, ((0,), (0,))).astype(jnp.bfloat16)
    stores.append(pltpu.make_async_copy(out_out, out_any, store_sem.at[2]))
    stores[2].start()

    for step in range(1, owners):
        t = lax.rem(me + owners - step, owners)
        remote(ret_buf.at[t], back_buf.at[t], rt_s.at[step], rt_r.at[t], me, other).wait_recv()
    returned = rows_of(back_buf[...])
    gathered = across(pick, returned[:, :head_dim], ((0,), (0,)))
    for h in range(heads):
        sub_out[:, h * head_dim : (h + 1) * head_dim] = gathered[
            h * positions : (h + 1) * positions
        ].astype(jnp.bfloat16)
    probs_out[...] = across(
        hits.astype(jnp.bfloat16), returned[:, head_dim:], ((0,), (0,))
    ).astype(jnp.bfloat16)
    for copy in sends:
        copy.wait_send()
    for store in stores:
        store.wait()


def fused(out_grad, merged, sub_tokens, routes, gate_probs, merge_weight, expert_in, expert_out):
    e_size, d_size = lax.axis_size("expert"), lax.axis_size("dp")
    owners = e_size * d_size
    length, feats = merged.shape[1:]
    positions, heads, head_dim = sub_tokens.shape[1:]
    top = routes.shape[3]
    count = positions * heads * top
    capacity = max(2, 3 * count // (2 * owners))
    wide = out_grad.shape[2]
    half_cols = wide // d_size
    half_units = expert_in.shape[2]
    padded = head_dim + LANES
    ids = routes[0].transpose(2, 1, 0).reshape(count)
    gates = gate_probs[0].transpose(2, 1, 0).reshape(1, count).astype(jnp.float32)
    low = jnp.bfloat16
    dma = pltpu.SemaphoreType.DMA
    vmem = pl.BlockSpec(memory_space=pltpu.VMEM)
    anywhere = pl.BlockSpec(memory_space=pl.ANY)
    one, two = dma((owners,)), dma((2 * owners,))
    merge_grad, grad_sub, probs, grad_in, grad_out = pl.pallas_call(
        functools.partial(layer_kernel, e_size, d_size, capacity, heads),
        out_shape=(
            jax.ShapeDtypeStruct(merge_weight.shape, low),
            jax.ShapeDtypeStruct((positions, wide), low),
            jax.ShapeDtypeStruct((count, LANES), low),
            jax.ShapeDtypeStruct((head_dim, half_units), low),
            jax.ShapeDtypeStruct((half_units, head_dim), low),
        ),
        in_specs=[vmem] * 6 + [anywhere] * 3,
        out_specs=(anywhere, vmem, vmem, anywhere, anywhere),
        scratch_shapes=[
            pltpu.VMEM(merge_weight.shape, low),
            pltpu.VMEM((head_dim, half_units), low),
            pltpu.VMEM((half_units, head_dim), low),
            pltpu.VMEM(merge_weight.shape, low),
            pltpu.VMEM((head_dim, half_units), low),
            pltpu.VMEM((half_units, head_dim), low),
            pltpu.VMEM((2, owners, positions, half_cols), low),
            pltpu.VMEM((d_size, length, feats), low),
            pltpu.VMEM((owners, capacity, padded), low),
            pltpu.VMEM((2, owners, capacity, padded), low),
            pltpu.VMEM((owners, capacity, head_dim), low),
            pltpu.VMEM((2, owners, capacity, head_dim), low),
            pltpu.VMEM((2, owners, positions, feats), low),
            pltpu.VMEM((2, owners, positions, feats), low),
            pltpu.VMEM((2, owners, capacity, padded), low),
            pltpu.VMEM((owners, capacity, padded), low),
            pltpu.VMEM((owners, capacity, padded), low),
            pltpu.VMEM((owners, capacity, padded), low),
            dma((4,)), dma((3,)),
            one, one, one, one,
            dma((d_size,)), dma((d_size,)),
            one, one, one, one,
            one, one, one, one,
            two, dma((2, owners)),
            one, one, one, one,
        ],
        compiler_params=pltpu.CompilerParams(
            collective_id=0, has_side_effects=True, vmem_limit_bytes=48 * 1024 * 1024
        ),
    )(
        ids.reshape(1, count), ids.reshape(count, 1), gates,
        out_grad[0], merged[0], sub_tokens[0].reshape(positions, wide),
        merge_weight, expert_in[0], expert_out[0],
    )
    grad_probs = probs[:, 0].reshape(top, heads, positions).transpose(2, 1, 0)
    return (
        merge_grad,
        grad_sub.reshape(sub_tokens.shape),
        grad_probs.reshape(gate_probs.shape),
        grad_in[None],
        grad_out[None],
    )


def fits(out_grad, merged, sub_tokens, routes, gate_probs, merge_weight, expert_in, expert_out):
    owners = lax.axis_size("expert") * lax.axis_size("dp")
    positions, heads, head_dim = sub_tokens.shape[1:]
    count = positions * heads * routes.shape[3]
    capacity = max(2, 3 * count // (2 * owners))
    return (
        lax.axis_size("pair") == 2
        and routes.shape[3] == 2
        and capacity % 8 == 0
        and positions % 16 == 0
        and head_dim % merged.shape[2] == 0
        and owners * positions <= 128
        and expert_in.shape[0] == 1
    )


def per_device(*arrays):
    if fits(*arrays):
        return fused(*arrays)
    return spread_plan(*arrays)


def solution(mesh):
    placed = (
        P(("groups", "dp"), ("expert", "pair"), None),
        P(("groups", "dp"), None, ("expert", "pair")),
        P(("groups", "dp"), ("expert", "pair"), None, None),
        P(("groups", "dp"), ("expert", "pair"), None, None),
        P(("groups", "dp"), ("expert", "pair"), None, None),
        P(("expert", "pair"), "dp"),
        P(("expert", "dp"), None, "pair"),
        P(("expert", "dp"), "pair", None),
    )
    return jax.shard_map(
        per_device,
        mesh=mesh,
        in_specs=placed,
        out_specs=(
            P(("groups", "expert", "pair"), "dp"),
            P(("groups", "dp"), ("expert", "pair"), None, None),
            P(("groups", "dp"), ("expert", "pair"), None, None),
            P(("groups", "expert", "dp"), None, "pair"),
            P(("groups", "expert", "dp"), "pair", None),
        ),
        check_vma=False,
    )
```

```python
import functools

import jax
import jax.numpy as jnp
from jax import lax
from jax.experimental import pallas as pl
from jax.experimental.pallas import tpu as pltpu
from jax.sharding import PartitionSpec as P


def expert_block(inputs, head_part, gates, first, second):
    preact = jnp.dot(inputs, first, preferred_element_type=jnp.float32)
    activated, pullback = jax.vjp(jax.nn.gelu, preact)
    back_hidden = lax.dot_general(
        head_part, second, (((1,), (1,)), ((), ())), preferred_element_type=jnp.float32
    )
    prob_half = jnp.sum(activated * back_hidden, axis=1)
    scales = gates.astype(jnp.float32)[:, None]
    hidden_grad = pullback(scales * back_hidden)[0].astype(jnp.bfloat16)
    out_scaled = (scales * head_part.astype(jnp.float32)).astype(jnp.bfloat16)
    act_low = activated.astype(jnp.bfloat16)
    grad_first = lax.dot_general(
        inputs, hidden_grad, (((0,), (0,)), ((), ())), preferred_element_type=jnp.float32
    )
    grad_second = lax.dot_general(
        act_low, out_scaled, (((0,), (0,)), ((), ())), preferred_element_type=jnp.float32
    )
    input_half = lax.dot_general(
        hidden_grad, first, (((1,), (1,)), ((), ())), preferred_element_type=jnp.float32
    )
    return (input_half, prob_half, grad_first, grad_second)


def slots_of(routes, experts, capacity):
    flat = routes.reshape(-1)
    top = routes.shape[-1]
    onehot = (flat[:, None] == jnp.arange(experts, dtype=jnp.int32)[None, :]).astype(jnp.int32)
    rank = jnp.sum((jnp.cumsum(onehot, axis=0) - onehot) * onehot, axis=1)
    return (flat * capacity + rank).reshape(-1, top)


def spread_plan(
    out_grad, merged, sub_tokens, routes, gate_probs, merge_weight, expert_in, expert_out
):
    experts = lax.axis_size("expert") * lax.axis_size("dp")
    data_size = lax.axis_size("dp")
    length, feats = merged.shape[1:]
    positions, head_count, head_dim = sub_tokens.shape[1:]
    top_count = routes.shape[3]
    subs = positions * head_count
    routed_count = subs * top_count
    capacity = max(2, 3 * routed_count // (2 * experts))
    slot_count = experts * capacity
    columns = lax.all_to_all(out_grad[0], "dp", split_axis=1, concat_axis=0, tiled=True)
    width = columns.shape[1]
    tokens = lax.all_gather(columns, ("expert", "pair"), axis=0, tiled=False)
    tokens = tokens.reshape(-1, data_size, positions, width).transpose(1, 0, 2, 3)
    tokens = tokens.reshape(data_size * length, width)
    saved = lax.all_gather(merged[0], "dp", axis=0, tiled=True)
    partial = lax.dot_general(
        tokens, merge_weight, (((1,), (1,)), ((), ())), preferred_element_type=jnp.float32
    ).reshape(data_size, length, feats)
    partial = lax.all_to_all(partial, "dp", split_axis=0, concat_axis=0, tiled=True)
    head_block = jnp.sum(partial, axis=0).astype(jnp.bfloat16)
    head_grad = lax.all_to_all(
        head_block, ("expert", "pair"), split_axis=0, concat_axis=1, tiled=True
    ).reshape(subs, head_dim)
    merge_grad = lax.dot_general(
        saved, tokens, (((0,), (0,)), ((), ())), preferred_element_type=jnp.float32
    ).astype(jnp.bfloat16)

    slots = slots_of(routes[0], experts, capacity)
    numbers = jnp.arange(slot_count, dtype=jnp.int32)
    hits = (slots[None, :, :] == numbers[:, None, None]).astype(jnp.bfloat16)
    pick = jnp.sum(hits, axis=2)
    gates = jnp.sum(
        hits.astype(jnp.float32)
        * gate_probs[0].reshape(1, subs, top_count).astype(jnp.float32),
        axis=(1, 2),
    ).astype(jnp.bfloat16)
    extra = jnp.broadcast_to(gates[:, None], (slot_count, 128))

    def select(rows):
        return jnp.dot(pick, rows, preferred_element_type=jnp.float32).astype(jnp.bfloat16)

    send_inputs = jnp.concatenate(
        [select(sub_tokens[0].reshape(subs, head_dim)), extra], axis=1
    ).reshape(experts, capacity, head_dim + 128)
    send_heads = select(head_grad).reshape(experts, capacity, head_dim)

    def spread(rows):
        got = lax.all_to_all(rows, ("expert", "dp"), split_axis=0, concat_axis=0, tiled=True)
        return lax.all_gather(got, "pair", axis=0, tiled=True).reshape(-1, rows.shape[2])

    inputs = spread(send_inputs)
    heads = spread(send_heads)
    first = expert_in[0]
    second = expert_out[0]
    input_part, prob_part, grads_first, grads_second = expert_block(
        inputs[:, :head_dim], heads, inputs[:, head_dim], first, second
    )
    both = jnp.concatenate(
        [input_part, jnp.broadcast_to(prob_part[:, None], (prob_part.shape[0], 128))], axis=1
    ).astype(jnp.bfloat16)
    summed = lax.psum_scatter(
        both.reshape(2 * experts, capacity, head_dim + 128),
        "pair",
        scatter_dimension=0,
        tiled=True,
    )
    back = lax.all_to_all(summed, ("expert", "dp"), split_axis=0, concat_axis=0, tiled=True)
    back = back.reshape(slot_count, head_dim + 128)
    grad_sub = lax.dot_general(
        pick, back[:, :head_dim], (((0,), (0,)), ((), ())), preferred_element_type=jnp.float32
    ).astype(jnp.bfloat16)
    grad_probs = jnp.sum(
        hits.astype(jnp.float32) * back[:, head_dim].astype(jnp.float32)[:, None, None], axis=0
    ).astype(jnp.bfloat16)
    return (
        merge_grad,
        grad_sub.reshape(sub_tokens.shape),
        grad_probs.reshape(gate_probs.shape),
        grads_first.astype(jnp.bfloat16).reshape(expert_in.shape),
        grads_second.astype(jnp.bfloat16).reshape(expert_out.shape),
    )


MESH = pl.DeviceIdType.MESH
LANES = 128


def across(left, right, dims):
    return lax.dot_general(left, right, ((dims[0], dims[1]), ((), ())), preferred_element_type=jnp.float32)


def rows_of(value):
    return value.astype(jnp.float32).reshape(-1, value.shape[-1]).astype(jnp.bfloat16)


def layer_kernel(
    e_size, d_size, capacity, heads,
    ids_any, gates_any, og_any, saved_any, subs, w_any, first_any, second_any,
    tokens_any, ordered_out, sub_out, probs_out, in_any, out_any,
    ids_in, gates_in, og, saved, w, first, second, in_out, out_out,
    og_buf, saved_buf, send_u, recv_u, send_g, recv_g, part_buf, home_buf, half_buf, pair_buf,
    ret_buf, back_buf,
    load_sem, store_sem, og_s, og_r, ogf_s, ogf_r, sv_s, sv_r, u_s, u_r, uf_s, uf_r, g_s, g_r, gf_s, gf_r,
    pt_s, pt_r, hf_s, hf_r, rt_s, rt_r,
):
    e, d, p = lax.axis_index("expert"), lax.axis_index("dp"), lax.axis_index("pair")
    owners = e_size * d_size
    me = e * d_size + d
    other = 1 - p
    positions, wide = og.shape
    half_cols = wide // d_size
    feats = saved.shape[1]
    head_dim = wide // heads
    slot_count = owners * capacity
    count = positions * heads * 2
    sub_rows = count // 2

    def in_row(ref):
        pieces = [ref[h, k : k + 1, :].astype(jnp.float32) for k in range(2) for h in range(heads)]
        return jnp.concatenate(pieces, axis=1)


    def place(t, q):
        return {"expert": t // d_size, "dp": lax.rem(t, d_size), "pair": q}

    def remote(src, dst, send, recv, t, q):
        return pltpu.make_async_remote_copy(
            src_ref=src, dst_ref=dst, send_sem=send, recv_sem=recv,
            device_id=place(t, q), device_id_type=MESH,
        )

    here = [
        pltpu.make_async_copy(og_any, og, load_sem.at[4]),
        pltpu.make_async_copy(saved_any, saved, load_sem.at[5]),
        pltpu.make_async_copy(ids_any, ids_in, load_sem.at[6]),
        pltpu.make_async_copy(gates_any, gates_in, load_sem.at[7]),
    ]
    loads = [
        pltpu.make_async_copy(w_any, w, load_sem.at[0]),
        pltpu.make_async_copy(first_any, first, load_sem.at[1]),
        pltpu.make_async_copy(second_any, second, load_sem.at[2]),
    ]
    for load in here + loads:
        load.start()

    barrier = pltpu.get_barrier_semaphore()
    mine = me * 2 + p
    for step in range(1, 2 * owners):
        q = lax.rem(mine + step, 2 * owners)
        pl.semaphore_signal(
            barrier, inc=1, device_id=place(q // 2, lax.rem(q, 2)), device_id_type=MESH
        )

    for load in here:
        load.wait()
    pl.semaphore_wait(barrier, 2 * owners - 1)

    sends = []

    def go(copy):
        copy.start()
        sends.append(copy)

    def columns(t):
        return og.at[:, pl.ds(pl.multiple_of(lax.rem(t, d_size) * half_cols, LANES), half_cols)]

    for step in range(1, owners):
        t = lax.rem(me + step, owners)
        go(remote(columns(t), og_buf.at[p, me], og_s.at[step], og_r.at[me], t, p))
    go(remote(columns(me), og_buf.at[p, me], ogf_s.at[me], ogf_r.at[me], me, other))
    own_og = pltpu.make_async_copy(columns(me), og_buf.at[p, me], load_sem.at[3])
    own_og.start()
    for step in range(1, d_size):
        t = e * d_size + lax.rem(d + step, d_size)
        go(remote(saved, saved_buf.at[d], sv_s.at[step], sv_r.at[d], t, p))
    saved_buf[d] = saved[...]
    rows_at = lax.broadcasted_iota(jnp.int32, (count, count), 0)
    lanes_at = lax.broadcasted_iota(jnp.int32, (count, count), 1)
    ids_row, gates_row = in_row(ids_in), in_row(gates_in)
    ids_col = jnp.sum(jnp.where(rows_at == lanes_at, ids_row, 0.0), axis=1, keepdims=True)
    rank = jnp.sum(
        jnp.where((rows_at < lanes_at) & (ids_col == ids_row), 1.0, 0.0), axis=0, keepdims=True
    )
    slots = (ids_row * capacity + rank).astype(jnp.int32)
    hits = jnp.where(
        lax.broadcasted_iota(jnp.int32, (slot_count, count), 0) == slots, 1.0, 0.0
    )
    pick = (hits[:, :sub_rows] + hits[:, sub_rows:]).astype(jnp.bfloat16)
    gate = jnp.sum(hits * gates_row, axis=1, keepdims=True)
    stacked = jnp.concatenate(
        [subs[:, h * head_dim : (h + 1) * head_dim] for h in range(heads)], axis=0
    )
    send_u[:, :, :head_dim] = (
        across(pick, stacked, ((1,), (0,))).reshape(owners, capacity, head_dim).astype(jnp.bfloat16)
    )
    send_u[:, :, head_dim:] = (
        jnp.broadcast_to(gate, (slot_count, LANES))
        .reshape(owners, capacity, LANES)
        .astype(jnp.bfloat16)
    )
    for step in range(1, owners):
        t = lax.rem(me + step, owners)
        go(remote(send_u.at[t], recv_u.at[p, me], u_s.at[step], u_r.at[me], t, p))
    go(remote(send_u.at[me], recv_u.at[p, me], uf_s.at[me], uf_r.at[me], me, other))
    recv_u[p, me] = send_u[me]

    def pass_on(buf, recv, fsend, frecv):
        for step in range(1, owners):
            t = lax.rem(me + owners - step, owners)
            remote(buf.at[p, t], buf.at[p, t], fsend.at[t], recv.at[t], me, other).wait_recv()
            go(remote(buf.at[p, t], buf.at[p, t], fsend.at[t], frecv.at[t], me, other))

    def from_pair(buf, fsend, frecv):
        for t in range(owners):
            remote(
                buf.at[other, t], buf.at[other, t], fsend.at[t], frecv.at[t], me, other
            ).wait_recv()

    pass_on(og_buf, og_r, ogf_s, ogf_r)
    own_og.wait()
    loads[0].wait()
    from_pair(og_buf, ogf_s, ogf_r)
    tokens = og_buf[...].reshape(2 * owners * positions, half_cols)
    part_buf[...] = (
        across(tokens, w[...], ((1,), (1,)))
        .astype(jnp.bfloat16)
        .reshape(2, owners, positions, feats)
    )
    for step in range(1, 2 * owners):
        q = lax.rem(mine + step, 2 * owners)
        t, qp = q // 2, lax.rem(q, 2)
        go(remote(part_buf.at[qp, t], home_buf.at[p, me], pt_s.at[step], pt_r.at[p, me], t, qp))
    home_buf[p, me] = part_buf[p, me]
    for step in range(1, 2 * owners):
        q = lax.rem(mine + 2 * owners - step, 2 * owners)
        t, qp = q // 2, lax.rem(q, 2)
        remote(
            home_buf.at[qp, t], home_buf.at[qp, t], pt_s.at[step], pt_r.at[qp, t], me, other
        ).wait_recv()
    blocks = []
    for i in range(e_size):
        for q in range(2):
            total = home_buf[q, i * d_size].astype(jnp.float32)
            for j in range(1, d_size):
                total = total + home_buf[q, i * d_size + j].astype(jnp.float32)
            blocks.append(total.astype(jnp.bfloat16))
    per_head = head_dim // feats
    head_rows = jnp.concatenate(
        [
            jnp.concatenate(blocks[h * per_head : (h + 1) * per_head], axis=1)
            for h in range(heads)
        ],
        axis=0,
    )
    send_g[...] = (
        across(pick, head_rows, ((1,), (0,)))
        .reshape(owners, capacity, head_dim)
        .astype(jnp.bfloat16)
    )
    for step in range(1, owners):
        t = lax.rem(me + step, owners)
        go(remote(send_g.at[t], recv_g.at[p, me], g_s.at[step], g_r.at[me], t, p))
    go(remote(send_g.at[me], recv_g.at[p, me], gf_s.at[me], gf_r.at[me], me, other))
    recv_g[p, me] = send_g[me]

    pass_on(recv_u, u_r, uf_s, uf_r)
    for step in range(1, d_size):
        j = lax.rem(d + step, d_size)
        remote(saved, saved_buf.at[j], sv_s.at[step], sv_r.at[j], me, other).wait_recv()
    ordered = jnp.concatenate(
        [
            saved_buf[j, (i * 2 + q) * positions : (i * 2 + q + 1) * positions, :]
            for q in range(2)
            for i in range(e_size)
            for j in range(d_size)
        ],
        axis=0,
    )
    ordered_out[...] = ordered
    stores = [pltpu.make_async_copy(og_buf, tokens_any, store_sem.at[0])]
    stores[0].start()
    from_pair(recv_u, uf_s, uf_r)
    inputs = rows_of(recv_u[:, :, :, :head_dim])
    scales = recv_u[:, :, :, head_dim:].astype(jnp.float32).reshape(-1, LANES)[:, :1]
    loads[1].wait()
    loads[2].wait()
    preact = across(inputs, first[...], ((1,), (0,)))
    root = 0.7978845608028654
    bend = jnp.tanh(root * (preact + 0.044715 * (preact * preact * preact)))
    activated = 0.5 * preact * (1.0 + bend)
    slope = 0.5 * (1.0 + bend) + 0.5 * preact * (1.0 - bend * bend) * (
        root * (1.0 + 3.0 * 0.044715 * (preact * preact))
    )

    pass_on(recv_g, g_r, gf_s, gf_r)
    from_pair(recv_g, gf_s, gf_r)
    grads = rows_of(recv_g[...])
    back = across(grads, second[...], ((1,), (1,)))
    hidden = (slope * (scales * back)).astype(jnp.bfloat16)
    half_buf[:, :, :, head_dim:] = (
        jnp.broadcast_to(
            jnp.sum(activated * back, axis=1, keepdims=True), (2 * slot_count, LANES)
        )
        .reshape(2, owners, capacity, LANES)
        .astype(jnp.bfloat16)
    )
    half_buf[:, :, :, :head_dim] = (
        across(hidden, first[...], ((1,), (1,)))
        .reshape(2, owners, capacity, head_dim)
        .astype(jnp.bfloat16)
    )
    order = [lax.rem(me + step, owners) for step in list(range(1, owners)) + [0]]
    for t in order:
        go(remote(half_buf.at[other, t], pair_buf.at[t], hf_s.at[t], hf_r.at[t], me, other))
    for step, t in enumerate(order):
        remote(half_buf.at[other, t], pair_buf.at[t], hf_s.at[t], hf_r.at[t], me, other).wait_recv()
        ret_buf[t] = (
            half_buf[p, t].astype(jnp.float32) + pair_buf[t].astype(jnp.float32)
        ).astype(jnp.bfloat16)
        if step < owners - 1:
            go(remote(ret_buf.at[t], back_buf.at[me], rt_s.at[step], rt_r.at[me], t, p))
    back_buf[me] = ret_buf[me]

    in_out[...] = across(inputs, hidden, ((0,), (0,))).astype(jnp.bfloat16)
    stores.append(pltpu.make_async_copy(in_out, in_any, store_sem.at[1]))
    stores[1].start()
    scaled = (scales * grads.astype(jnp.float32)).astype(jnp.bfloat16)
    out_out[...] = across(activated.astype(jnp.bfloat16), scaled, ((0,), (0,))).astype(jnp.bfloat16)
    stores.append(pltpu.make_async_copy(out_out, out_any, store_sem.at[2]))
    stores[2].start()

    for step in range(1, owners):
        t = lax.rem(me + owners - step, owners)
        remote(ret_buf.at[t], back_buf.at[t], rt_s.at[step], rt_r.at[t], me, other).wait_recv()
    returned = rows_of(back_buf[...])
    gathered = across(pick, returned[:, :head_dim], ((0,), (0,)))
    for h in range(heads):
        sub_out[:, h * head_dim : (h + 1) * head_dim] = gathered[
            h * positions : (h + 1) * positions
        ].astype(jnp.bfloat16)
    probs = jnp.sum(hits * returned[:, head_dim:].astype(jnp.float32), axis=0, keepdims=True)
    for k in range(2):
        for h in range(heads):
            at = (k * heads + h) * positions
            probs_out[h, k : k + 1, :] = probs[:, at : at + positions].astype(jnp.bfloat16)
    for copy in sends:
        copy.wait_send()
    for store in stores:
        store.wait()


def fused(out_grad, merged, sub_tokens, routes, gate_probs, merge_weight, expert_in, expert_out):
    e_size, d_size = lax.axis_size("expert"), lax.axis_size("dp")
    owners = e_size * d_size
    length, feats = merged.shape[1:]
    positions, heads, head_dim = sub_tokens.shape[1:]
    top = routes.shape[3]
    count = positions * heads * top
    capacity = max(2, 3 * count // (2 * owners))
    wide = out_grad.shape[2]
    half_cols = wide // d_size
    half_units = expert_in.shape[2]
    padded = head_dim + LANES
    low = jnp.bfloat16
    dma = pltpu.SemaphoreType.DMA
    vmem = pl.BlockSpec(memory_space=pltpu.VMEM)
    anywhere = pl.BlockSpec(memory_space=pl.ANY)
    def held(value):
        return pltpu.with_memory_space_constraint(value, pltpu.HBM)

    one, two = dma((owners,)), dma((2 * owners,))
    tokens, ordered, grad_sub, probs, grad_in, grad_out = pl.pallas_call(
        functools.partial(layer_kernel, e_size, d_size, capacity, heads),
        out_shape=(
            jax.ShapeDtypeStruct((2, owners, positions, half_cols), low),
            jax.ShapeDtypeStruct((2 * owners * positions, feats), low),
            jax.ShapeDtypeStruct((positions, wide), low),
            jax.ShapeDtypeStruct((heads, top, positions), low),
            jax.ShapeDtypeStruct((head_dim, half_units), low),
            jax.ShapeDtypeStruct((half_units, head_dim), low),
        ),
        in_specs=[anywhere] * 4 + [vmem] + [anywhere] * 3,
        out_specs=(anywhere, vmem, vmem, vmem, anywhere, anywhere),
        scratch_shapes=[
            pltpu.VMEM((heads, top, positions), jnp.int32),
            pltpu.VMEM((heads, top, positions), low),
            pltpu.VMEM((positions, wide), low),
            pltpu.VMEM((length, feats), low),
            pltpu.VMEM(merge_weight.shape, low),
            pltpu.VMEM((head_dim, half_units), low),
            pltpu.VMEM((half_units, head_dim), low),
            pltpu.VMEM((head_dim, half_units), low),
            pltpu.VMEM((half_units, head_dim), low),
            pltpu.VMEM((2, owners, positions, half_cols), low),
            pltpu.VMEM((d_size, length, feats), low),
            pltpu.VMEM((owners, capacity, padded), low),
            pltpu.VMEM((2, owners, capacity, padded), low),
            pltpu.VMEM((owners, capacity, head_dim), low),
            pltpu.VMEM((2, owners, capacity, head_dim), low),
            pltpu.VMEM((2, owners, positions, feats), low),
            pltpu.VMEM((2, owners, positions, feats), low),
            pltpu.VMEM((2, owners, capacity, padded), low),
            pltpu.VMEM((owners, capacity, padded), low),
            pltpu.VMEM((owners, capacity, padded), low),
            pltpu.VMEM((owners, capacity, padded), low),
            dma((8,)), dma((3,)),
            one, one, one, one,
            dma((d_size,)), dma((d_size,)),
            one, one, one, one,
            one, one, one, one,
            two, dma((2, owners)),
            one, one, one, one,
        ],
        compiler_params=pltpu.CompilerParams(
            collective_id=0, has_side_effects=True, vmem_limit_bytes=48 * 1024 * 1024
        ),
    )(
        held(routes[0].transpose(1, 2, 0)), held(gate_probs[0].transpose(1, 2, 0)),
        held(out_grad[0]), held(merged[0]), sub_tokens[0].reshape(positions, wide),
        held(merge_weight), held(expert_in[0]), held(expert_out[0]),
    )
    merge_grad = across(
        ordered, tokens.reshape(2 * owners * positions, half_cols), ((0,), (0,))
    ).astype(low)
    grad_probs = probs.transpose(2, 0, 1)
    return (
        merge_grad,
        grad_sub.reshape(sub_tokens.shape),
        grad_probs.reshape(gate_probs.shape),
        grad_in[None],
        grad_out[None],
    )


def fits(out_grad, merged, sub_tokens, routes, gate_probs, merge_weight, expert_in, expert_out):
    owners = lax.axis_size("expert") * lax.axis_size("dp")
    positions, heads, head_dim = sub_tokens.shape[1:]
    count = positions * heads * routes.shape[3]
    capacity = max(2, 3 * count // (2 * owners))
    return (
        lax.axis_size("pair") == 2
        and routes.shape[3] == 2
        and capacity % 8 == 0
        and positions % 16 == 0
        and head_dim % merged.shape[2] == 0
        and owners * positions <= 128
        and expert_in.shape[0] == 1
    )


def per_device(*arrays):
    if fits(*arrays):
        return fused(*arrays)
    return spread_plan(*arrays)


def solution(mesh):
    placed = (
        P(("groups", "dp"), ("expert", "pair"), None),
        P(("groups", "dp"), None, ("expert", "pair")),
        P(("groups", "dp"), ("expert", "pair"), None, None),
        P(("groups", "dp"), ("expert", "pair"), None, None),
        P(("groups", "dp"), ("expert", "pair"), None, None),
        P(("expert", "pair"), "dp"),
        P(("expert", "dp"), None, "pair"),
        P(("expert", "dp"), "pair", None),
    )
    return jax.shard_map(
        per_device,
        mesh=mesh,
        in_specs=placed,
        out_specs=(
            P(("groups", "expert", "pair"), "dp"),
            P(("groups", "dp"), ("expert", "pair"), None, None),
            P(("groups", "dp"), ("expert", "pair"), None, None),
            P(("groups", "expert", "dp"), None, "pair"),
            P(("groups", "expert", "dp"), "pair", None),
        ),
        check_vma=False,
    )
```

```python
import functools

import jax
import jax.numpy as jnp
from jax import lax
from jax.experimental import pallas as pl
from jax.experimental.pallas import tpu as pltpu
from jax.sharding import PartitionSpec as P


def expert_block(inputs, head_part, gates, first, second):
    preact = jnp.dot(inputs, first, preferred_element_type=jnp.float32)
    activated, pullback = jax.vjp(jax.nn.gelu, preact)
    back_hidden = lax.dot_general(
        head_part, second, (((1,), (1,)), ((), ())), preferred_element_type=jnp.float32
    )
    prob_half = jnp.sum(activated * back_hidden, axis=1)
    scales = gates.astype(jnp.float32)[:, None]
    hidden_grad = pullback(scales * back_hidden)[0].astype(jnp.bfloat16)
    out_scaled = (scales * head_part.astype(jnp.float32)).astype(jnp.bfloat16)
    act_low = activated.astype(jnp.bfloat16)
    grad_first = lax.dot_general(
        inputs, hidden_grad, (((0,), (0,)), ((), ())), preferred_element_type=jnp.float32
    )
    grad_second = lax.dot_general(
        act_low, out_scaled, (((0,), (0,)), ((), ())), preferred_element_type=jnp.float32
    )
    input_half = lax.dot_general(
        hidden_grad, first, (((1,), (1,)), ((), ())), preferred_element_type=jnp.float32
    )
    return (input_half, prob_half, grad_first, grad_second)


def slots_of(routes, experts, capacity):
    flat = routes.reshape(-1)
    top = routes.shape[-1]
    onehot = (flat[:, None] == jnp.arange(experts, dtype=jnp.int32)[None, :]).astype(jnp.int32)
    rank = jnp.sum((jnp.cumsum(onehot, axis=0) - onehot) * onehot, axis=1)
    return (flat * capacity + rank).reshape(-1, top)


def spread_plan(
    out_grad, merged, sub_tokens, routes, gate_probs, merge_weight, expert_in, expert_out
):
    experts = lax.axis_size("expert") * lax.axis_size("dp")
    data_size = lax.axis_size("dp")
    length, feats = merged.shape[1:]
    positions, head_count, head_dim = sub_tokens.shape[1:]
    top_count = routes.shape[3]
    subs = positions * head_count
    routed_count = subs * top_count
    capacity = max(2, 3 * routed_count // (2 * experts))
    slot_count = experts * capacity
    columns = lax.all_to_all(out_grad[0], "dp", split_axis=1, concat_axis=0, tiled=True)
    width = columns.shape[1]
    tokens = lax.all_gather(columns, ("expert", "pair"), axis=0, tiled=False)
    tokens = tokens.reshape(-1, data_size, positions, width).transpose(1, 0, 2, 3)
    tokens = tokens.reshape(data_size * length, width)
    saved = lax.all_gather(merged[0], "dp", axis=0, tiled=True)
    partial = lax.dot_general(
        tokens, merge_weight, (((1,), (1,)), ((), ())), preferred_element_type=jnp.float32
    ).reshape(data_size, length, feats)
    partial = lax.all_to_all(partial, "dp", split_axis=0, concat_axis=0, tiled=True)
    head_block = jnp.sum(partial, axis=0).astype(jnp.bfloat16)
    head_grad = lax.all_to_all(
        head_block, ("expert", "pair"), split_axis=0, concat_axis=1, tiled=True
    ).reshape(subs, head_dim)
    merge_grad = lax.dot_general(
        saved, tokens, (((0,), (0,)), ((), ())), preferred_element_type=jnp.float32
    ).astype(jnp.bfloat16)

    slots = slots_of(routes[0], experts, capacity)
    numbers = jnp.arange(slot_count, dtype=jnp.int32)
    hits = (slots[None, :, :] == numbers[:, None, None]).astype(jnp.bfloat16)
    pick = jnp.sum(hits, axis=2)
    gates = jnp.sum(
        hits.astype(jnp.float32)
        * gate_probs[0].reshape(1, subs, top_count).astype(jnp.float32),
        axis=(1, 2),
    ).astype(jnp.bfloat16)
    extra = jnp.broadcast_to(gates[:, None], (slot_count, 128))

    def select(rows):
        return jnp.dot(pick, rows, preferred_element_type=jnp.float32).astype(jnp.bfloat16)

    send_inputs = jnp.concatenate(
        [select(sub_tokens[0].reshape(subs, head_dim)), extra], axis=1
    ).reshape(experts, capacity, head_dim + 128)
    send_heads = select(head_grad).reshape(experts, capacity, head_dim)

    def spread(rows):
        got = lax.all_to_all(rows, ("expert", "dp"), split_axis=0, concat_axis=0, tiled=True)
        return lax.all_gather(got, "pair", axis=0, tiled=True).reshape(-1, rows.shape[2])

    inputs = spread(send_inputs)
    heads = spread(send_heads)
    first = expert_in[0]
    second = expert_out[0]
    input_part, prob_part, grads_first, grads_second = expert_block(
        inputs[:, :head_dim], heads, inputs[:, head_dim], first, second
    )
    both = jnp.concatenate(
        [input_part, jnp.broadcast_to(prob_part[:, None], (prob_part.shape[0], 128))], axis=1
    ).astype(jnp.bfloat16)
    summed = lax.psum_scatter(
        both.reshape(2 * experts, capacity, head_dim + 128),
        "pair",
        scatter_dimension=0,
        tiled=True,
    )
    back = lax.all_to_all(summed, ("expert", "dp"), split_axis=0, concat_axis=0, tiled=True)
    back = back.reshape(slot_count, head_dim + 128)
    grad_sub = lax.dot_general(
        pick, back[:, :head_dim], (((0,), (0,)), ((), ())), preferred_element_type=jnp.float32
    ).astype(jnp.bfloat16)
    grad_probs = jnp.sum(
        hits.astype(jnp.float32) * back[:, head_dim].astype(jnp.float32)[:, None, None], axis=0
    ).astype(jnp.bfloat16)
    return (
        merge_grad,
        grad_sub.reshape(sub_tokens.shape),
        grad_probs.reshape(gate_probs.shape),
        grads_first.astype(jnp.bfloat16).reshape(expert_in.shape),
        grads_second.astype(jnp.bfloat16).reshape(expert_out.shape),
    )


MESH = pl.DeviceIdType.MESH
LANES = 128


def across(left, right, dims):
    return lax.dot_general(left, right, ((dims[0], dims[1]), ((), ())), preferred_element_type=jnp.float32)


def rows_of(value):
    return value.astype(jnp.float32).reshape(-1, value.shape[-1]).astype(jnp.bfloat16)


def layer_kernel(
    e_size, d_size, capacity, heads,
    ids_any, gates_any, og_any, saved_any, subs, w_any, first_any, second_any,
    tokens_any, ordered_out, sub_out, probs_out, in_any, out_any,
    ids_in, gates_in, og, saved, w, first, second, in_out, out_out, part_own, x_send, x_recv,
    og_buf, saved_buf, send_u, recv_u, send_g, recv_g, part_buf, home_buf, half_buf, pair_buf,
    ret_buf, back_buf,
    load_sem, store_sem, x_s, x_r, og_s, og_r, ogf_s, ogf_r, sv_s, sv_r, u_s, u_r, uf_s, uf_r, g_s, g_r, gf_s, gf_r,
    pt_s, pt_r, hf_s, hf_r, rt_s, rt_r,
):
    e, d, p = lax.axis_index("expert"), lax.axis_index("dp"), lax.axis_index("pair")
    owners = e_size * d_size
    me = e * d_size + d
    other = 1 - p
    positions, wide = og.shape
    half_cols = wide // d_size
    feats = saved.shape[1]
    head_dim = wide // heads
    slot_count = owners * capacity
    count = positions * heads * 2
    sub_rows = count // 2

    def in_row(ref):
        pieces = [ref[h, k : k + 1, :].astype(jnp.float32) for k in range(2) for h in range(heads)]
        return jnp.concatenate(pieces, axis=1)


    def place(t, q):
        return {"expert": t // d_size, "dp": lax.rem(t, d_size), "pair": q}

    def remote(src, dst, send, recv, t, q):
        return pltpu.make_async_remote_copy(
            src_ref=src, dst_ref=dst, send_sem=send, recv_sem=recv,
            device_id=place(t, q), device_id_type=MESH,
        )

    here = [
        pltpu.make_async_copy(og_any, og, load_sem.at[4]),
        pltpu.make_async_copy(saved_any, saved, load_sem.at[5]),
        pltpu.make_async_copy(ids_any, ids_in, load_sem.at[6]),
        pltpu.make_async_copy(gates_any, gates_in, load_sem.at[7]),
    ]
    loads = [
        pltpu.make_async_copy(w_any, w, load_sem.at[0]),
        pltpu.make_async_copy(first_any, first, load_sem.at[1]),
        pltpu.make_async_copy(second_any, second, load_sem.at[2]),
    ]
    for load in here + loads:
        load.start()

    barrier = pltpu.get_barrier_semaphore()
    mine = me * 2 + p
    for step in range(1, 2 * owners):
        q = lax.rem(mine + step, 2 * owners)
        pl.semaphore_signal(
            barrier, inc=1, device_id=place(q // 2, lax.rem(q, 2)), device_id_type=MESH
        )

    for load in here:
        load.wait()
    pl.semaphore_wait(barrier, 2 * owners - 1)

    sends = []

    def go(copy):
        copy.start()
        sends.append(copy)

    def columns(t):
        return og.at[:, pl.ds(pl.multiple_of(lax.rem(t, d_size) * half_cols, LANES), half_cols)]

    for step in range(1, owners):
        t = lax.rem(me + step, owners)
        go(remote(columns(t), og_buf.at[p, me], og_s.at[step], og_r.at[me], t, p))
    go(remote(columns(me), og_buf.at[p, me], ogf_s.at[me], ogf_r.at[me], me, other))
    own_og = pltpu.make_async_copy(columns(me), og_buf.at[p, me], load_sem.at[3])
    own_og.start()
    for step in range(1, d_size):
        t = e * d_size + lax.rem(d + step, d_size)
        go(remote(saved, saved_buf.at[d], sv_s.at[step], sv_r.at[d], t, p))
    saved_buf[d] = saved[...]
    rows_at = lax.broadcasted_iota(jnp.int32, (count, count), 0)
    lanes_at = lax.broadcasted_iota(jnp.int32, (count, count), 1)
    ids_row, gates_row = in_row(ids_in), in_row(gates_in)
    ids_col = jnp.sum(jnp.where(rows_at == lanes_at, ids_row, 0.0), axis=1, keepdims=True)
    rank = jnp.sum(
        jnp.where((rows_at < lanes_at) & (ids_col == ids_row), 1.0, 0.0), axis=0, keepdims=True
    )
    slots = (ids_row * capacity + rank).astype(jnp.int32)
    hits = jnp.where(
        lax.broadcasted_iota(jnp.int32, (slot_count, count), 0) == slots, 1.0, 0.0
    )
    pick = (hits[:, :sub_rows] + hits[:, sub_rows:]).astype(jnp.bfloat16)
    gate = jnp.sum(hits * gates_row, axis=1, keepdims=True)
    stacked = jnp.concatenate(
        [subs[:, h * head_dim : (h + 1) * head_dim] for h in range(heads)], axis=0
    )
    send_u[:, :, :head_dim] = (
        across(pick, stacked, ((1,), (0,))).reshape(owners, capacity, head_dim).astype(jnp.bfloat16)
    )
    send_u[:, :, head_dim:] = (
        jnp.broadcast_to(gate, (slot_count, LANES))
        .reshape(owners, capacity, LANES)
        .astype(jnp.bfloat16)
    )
    for step in range(1, 4):
        t = lax.rem(me + step, owners)
        go(remote(send_u.at[t], recv_u.at[p, me], u_s.at[step], u_r.at[me], t, p))
    recv_u[p, me] = send_u[me]

    def pass_on(buf, recv, fsend, frecv):
        for step in range(1, owners):
            t = lax.rem(me + owners - step, owners)
            remote(buf.at[p, t], buf.at[p, t], fsend.at[t], recv.at[t], me, other).wait_recv()
            go(remote(buf.at[p, t], buf.at[p, t], fsend.at[t], frecv.at[t], me, other))

    def from_pair(buf, fsend, frecv):
        for t in range(owners):
            remote(
                buf.at[other, t], buf.at[other, t], fsend.at[t], frecv.at[t], me, other
            ).wait_recv()

    pass_on(og_buf, og_r, ogf_s, ogf_r)
    own_og.wait()
    loads[0].wait()
    from_pair(og_buf, ogf_s, ogf_r)
    tokens = og_buf[...].reshape(2 * owners * positions, half_cols)
    partial = across(tokens, w[...], ((1,), (1,))).reshape(
        2 * e_size, d_size, positions, feats
    )
    for j in range(d_size):
        x_send[j] = partial[:, j].astype(jnp.bfloat16)
        part_own[j] = partial[:, j]
    for step in range(1, d_size):
        j = lax.rem(d + step, d_size)
        go(remote(x_send.at[j], x_recv.at[d], x_s.at[step], x_r.at[d], e * d_size + j, p))
    for step in range(4, owners):
        t = lax.rem(me + step, owners)
        go(remote(send_u.at[t], recv_u.at[p, me], u_s.at[step], u_r.at[me], t, p))
    go(remote(send_u.at[me], recv_u.at[p, me], uf_s.at[me], uf_r.at[me], me, other))
    total = part_own[d]
    for step in range(1, d_size):
        j = lax.rem(d + d_size - step, d_size)
        remote(x_recv.at[j], x_recv.at[j], x_s.at[step], x_r.at[j], me, other).wait_recv()
        total = total + x_recv[j].astype(jnp.float32)
    part_buf[...] = total.astype(jnp.bfloat16).reshape(2, e_size, positions, feats)
    spot = e * 2 + p
    for step in range(1, 2 * e_size):
        n = lax.rem(spot + step, 2 * e_size)
        i, q = n // 2, lax.rem(n, 2)
        go(
            remote(
                part_buf.at[q, i], home_buf.at[p, e], pt_s.at[step], pt_r.at[p, e],
                i * d_size + d, q,
            )
        )
    home_buf[p, e] = part_buf[p, e]
    for step in range(1, 2 * e_size):
        n = lax.rem(spot + 2 * e_size - step, 2 * e_size)
        i, q = n // 2, lax.rem(n, 2)
        remote(
            home_buf.at[q, i], home_buf.at[q, i], pt_s.at[step], pt_r.at[q, i], me, other
        ).wait_recv()
    blocks = [home_buf[q, i] for i in range(e_size) for q in range(2)]
    per_head = head_dim // feats
    head_rows = jnp.concatenate(
        [
            jnp.concatenate(blocks[h * per_head : (h + 1) * per_head], axis=1)
            for h in range(heads)
        ],
        axis=0,
    )
    send_g[...] = (
        across(pick, head_rows, ((1,), (0,)))
        .reshape(owners, capacity, head_dim)
        .astype(jnp.bfloat16)
    )
    for step in range(1, owners):
        t = lax.rem(me + step, owners)
        go(remote(send_g.at[t], recv_g.at[p, me], g_s.at[step], g_r.at[me], t, p))
    go(remote(send_g.at[me], recv_g.at[p, me], gf_s.at[me], gf_r.at[me], me, other))
    recv_g[p, me] = send_g[me]

    pass_on(recv_u, u_r, uf_s, uf_r)
    for step in range(1, d_size):
        j = lax.rem(d + step, d_size)
        remote(saved, saved_buf.at[j], sv_s.at[step], sv_r.at[j], me, other).wait_recv()
    ordered = jnp.concatenate(
        [
            saved_buf[j, (i * 2 + q) * positions : (i * 2 + q + 1) * positions, :]
            for q in range(2)
            for i in range(e_size)
            for j in range(d_size)
        ],
        axis=0,
    )
    ordered_out[...] = ordered
    stores = [pltpu.make_async_copy(og_buf, tokens_any, store_sem.at[0])]
    stores[0].start()
    from_pair(recv_u, uf_s, uf_r)
    inputs = rows_of(recv_u[:, :, :, :head_dim])
    scales = recv_u[:, :, :, head_dim:].astype(jnp.float32).reshape(-1, LANES)[:, :1]
    loads[1].wait()
    loads[2].wait()
    preact = across(inputs, first[...], ((1,), (0,)))
    root = 0.7978845608028654
    bend = jnp.tanh(root * (preact + 0.044715 * (preact * preact * preact)))
    activated = 0.5 * preact * (1.0 + bend)
    slope = 0.5 * (1.0 + bend) + 0.5 * preact * (1.0 - bend * bend) * (
        root * (1.0 + 3.0 * 0.044715 * (preact * preact))
    )

    pass_on(recv_g, g_r, gf_s, gf_r)
    from_pair(recv_g, gf_s, gf_r)
    grads = rows_of(recv_g[...])
    back = across(grads, second[...], ((1,), (1,)))
    hidden = (slope * (scales * back)).astype(jnp.bfloat16)
    half_buf[:, :, :, head_dim:] = (
        jnp.broadcast_to(
            jnp.sum(activated * back, axis=1, keepdims=True), (2 * slot_count, LANES)
        )
        .reshape(2, owners, capacity, LANES)
        .astype(jnp.bfloat16)
    )
    half_buf[:, :, :, :head_dim] = (
        across(hidden, first[...], ((1,), (1,)))
        .reshape(2, owners, capacity, head_dim)
        .astype(jnp.bfloat16)
    )
    order = [lax.rem(me + step, owners) for step in list(range(1, owners)) + [0]]
    for t in order:
        go(remote(half_buf.at[other, t], pair_buf.at[t], hf_s.at[t], hf_r.at[t], me, other))
    for step, t in enumerate(order):
        remote(half_buf.at[other, t], pair_buf.at[t], hf_s.at[t], hf_r.at[t], me, other).wait_recv()
        ret_buf[t] = (
            half_buf[p, t].astype(jnp.float32) + pair_buf[t].astype(jnp.float32)
        ).astype(jnp.bfloat16)
        if step < owners - 1:
            go(remote(ret_buf.at[t], back_buf.at[me], rt_s.at[step], rt_r.at[me], t, p))
    back_buf[me] = ret_buf[me]

    in_out[...] = across(inputs, hidden, ((0,), (0,))).astype(jnp.bfloat16)
    stores.append(pltpu.make_async_copy(in_out, in_any, store_sem.at[1]))
    stores[1].start()
    scaled = (scales * grads.astype(jnp.float32)).astype(jnp.bfloat16)
    out_out[...] = across(activated.astype(jnp.bfloat16), scaled, ((0,), (0,))).astype(jnp.bfloat16)
    stores.append(pltpu.make_async_copy(out_out, out_any, store_sem.at[2]))
    stores[2].start()

    for step in range(1, owners):
        t = lax.rem(me + owners - step, owners)
        remote(ret_buf.at[t], back_buf.at[t], rt_s.at[step], rt_r.at[t], me, other).wait_recv()
    returned = rows_of(back_buf[...])
    gathered = across(pick, returned[:, :head_dim], ((0,), (0,)))
    for h in range(heads):
        sub_out[:, h * head_dim : (h + 1) * head_dim] = gathered[
            h * positions : (h + 1) * positions
        ].astype(jnp.bfloat16)
    probs = jnp.sum(hits * returned[:, head_dim:].astype(jnp.float32), axis=0, keepdims=True)
    for k in range(2):
        for h in range(heads):
            at = (k * heads + h) * positions
            probs_out[h, k : k + 1, :] = probs[:, at : at + positions].astype(jnp.bfloat16)
    for copy in sends:
        copy.wait_send()
    for store in stores:
        store.wait()


def finish_kernel(
    chunk, heads, ordered, tokens, sub, probs_any, in_any, out_any,
    merge_to, sub_out, probs_to, in_to, out_to, merge_buf, sem, chunk_sem,
):
    copies = [
        pltpu.make_async_copy(in_any, in_to, sem.at[0]),
        pltpu.make_async_copy(out_any, out_to, sem.at[1]),
        pltpu.make_async_copy(probs_any, probs_to, sem.at[2]),
    ]
    for copy in copies:
        copy.start()
    rows = tokens.shape[0] * tokens.shape[1] * tokens.shape[2]
    for c in range(tokens.shape[3] // chunk):
        at = pl.ds(c * chunk, chunk)
        merge_buf[c] = across(
            ordered[...], tokens[:, :, :, at].reshape(rows, chunk), ((0,), (0,))
        ).astype(jnp.bfloat16)
        copies.append(pltpu.make_async_copy(merge_buf.at[c], merge_to.at[:, at], chunk_sem.at[c]))
        copies[-1].start()
    width = sub.shape[1] // heads
    for h in range(heads):
        sub_out[:, h, :] = sub[:, h * width : (h + 1) * width]
    for copy in copies:
        copy.wait()


def fused(out_grad, merged, sub_tokens, routes, gate_probs, merge_weight, expert_in, expert_out):
    e_size, d_size = lax.axis_size("expert"), lax.axis_size("dp")
    owners = e_size * d_size
    length, feats = merged.shape[1:]
    positions, heads, head_dim = sub_tokens.shape[1:]
    top = routes.shape[3]
    count = positions * heads * top
    capacity = max(2, 3 * count // (2 * owners))
    wide = out_grad.shape[2]
    half_cols = wide // d_size
    half_units = expert_in.shape[2]
    padded = head_dim + LANES
    low = jnp.bfloat16
    dma = pltpu.SemaphoreType.DMA
    vmem = pl.BlockSpec(memory_space=pltpu.VMEM)
    anywhere = pl.BlockSpec(memory_space=pl.ANY)
    def held(value):
        return pltpu.with_memory_space_constraint(value, pltpu.HBM)

    one, two = dma((owners,)), dma((2 * owners,))
    tokens, ordered, grad_sub, probs, grad_in, grad_out = pl.pallas_call(
        functools.partial(layer_kernel, e_size, d_size, capacity, heads),
        out_shape=(
            jax.ShapeDtypeStruct((2, owners, positions, half_cols), low),
            jax.ShapeDtypeStruct((2 * owners * positions, feats), low),
            jax.ShapeDtypeStruct((positions, wide), low),
            jax.ShapeDtypeStruct((heads, top, positions), low),
            jax.ShapeDtypeStruct((head_dim, half_units), low),
            jax.ShapeDtypeStruct((half_units, head_dim), low),
        ),
        in_specs=[anywhere] * 4 + [vmem] + [anywhere] * 3,
        out_specs=(anywhere, vmem, vmem, vmem, anywhere, anywhere),
        scratch_shapes=[
            pltpu.VMEM((heads, top, positions), jnp.int32),
            pltpu.VMEM((heads, top, positions), low),
            pltpu.VMEM((positions, wide), low),
            pltpu.VMEM((length, feats), low),
            pltpu.VMEM(merge_weight.shape, low),
            pltpu.VMEM((head_dim, half_units), low),
            pltpu.VMEM((half_units, head_dim), low),
            pltpu.VMEM((head_dim, half_units), low),
            pltpu.VMEM((half_units, head_dim), low),
            pltpu.VMEM((d_size, 2 * e_size, positions, feats), jnp.float32),
            pltpu.VMEM((d_size, 2 * e_size, positions, feats), low),
            pltpu.VMEM((d_size, 2 * e_size, positions, feats), low),
            pltpu.VMEM((2, owners, positions, half_cols), low),
            pltpu.VMEM((d_size, length, feats), low),
            pltpu.VMEM((owners, capacity, padded), low),
            pltpu.VMEM((2, owners, capacity, padded), low),
            pltpu.VMEM((owners, capacity, head_dim), low),
            pltpu.VMEM((2, owners, capacity, head_dim), low),
            pltpu.VMEM((2, e_size, positions, feats), low),
            pltpu.VMEM((2, e_size, positions, feats), low),
            pltpu.VMEM((2, owners, capacity, padded), low),
            pltpu.VMEM((owners, capacity, padded), low),
            pltpu.VMEM((owners, capacity, padded), low),
            pltpu.VMEM((owners, capacity, padded), low),
            dma((8,)), dma((3,)), dma((d_size,)), dma((d_size,)),
            one, one, one, one,
            dma((d_size,)), dma((d_size,)),
            one, one, one, one,
            one, one, one, one,
            two, dma((2, e_size)),
            one, one, one, one,
        ],
        compiler_params=pltpu.CompilerParams(
            collective_id=0, has_side_effects=True, vmem_limit_bytes=48 * 1024 * 1024
        ),
    )(
        held(routes[0].transpose(1, 2, 0)), held(gate_probs[0].transpose(1, 2, 0)),
        held(out_grad[0]), held(merged[0]), sub_tokens[0].reshape(positions, wide),
        held(merge_weight), held(expert_in[0]), held(expert_out[0]),
    )
    chunk = half_cols // 4
    shape_of = jax.ShapeDtypeStruct
    merge_grad, grad_sub, probs, grad_in, grad_out = pl.pallas_call(
        functools.partial(finish_kernel, chunk, heads),
        out_shape=(
            shape_of(merge_weight.shape, low),
            shape_of((positions, heads, head_dim), low),
            shape_of(probs.shape, low),
            shape_of(grad_in.shape, low),
            shape_of(grad_out.shape, low),
        ),
        in_specs=[vmem] * 3 + [anywhere] * 3,
        out_specs=(anywhere, vmem, anywhere, anywhere, anywhere),
        scratch_shapes=[pltpu.VMEM((4, feats, chunk), low), dma((3,)), dma((4,))],
        compiler_params=pltpu.CompilerParams(vmem_limit_bytes=16 * 1024 * 1024),
    )(ordered, tokens, grad_sub, probs, grad_in, grad_out)
    grad_probs = probs.transpose(2, 0, 1)
    return (
        merge_grad,
        grad_sub.reshape(sub_tokens.shape),
        grad_probs.reshape(gate_probs.shape),
        grad_in[None],
        grad_out[None],
    )


def fits(out_grad, merged, sub_tokens, routes, gate_probs, merge_weight, expert_in, expert_out):
    owners = lax.axis_size("expert") * lax.axis_size("dp")
    positions, heads, head_dim = sub_tokens.shape[1:]
    count = positions * heads * routes.shape[3]
    capacity = max(2, 3 * count // (2 * owners))
    return (
        lax.axis_size("pair") == 2
        and routes.shape[3] == 2
        and capacity % 8 == 0
        and positions % 16 == 0
        and head_dim % merged.shape[2] == 0
        and owners * positions <= 128
        and expert_in.shape[0] == 1
    )


def per_device(*arrays):
    if fits(*arrays):
        return fused(*arrays)
    return spread_plan(*arrays)


def solution(mesh):
    placed = (
        P(("groups", "dp"), ("expert", "pair"), None),
        P(("groups", "dp"), None, ("expert", "pair")),
        P(("groups", "dp"), ("expert", "pair"), None, None),
        P(("groups", "dp"), ("expert", "pair"), None, None),
        P(("groups", "dp"), ("expert", "pair"), None, None),
        P(("expert", "pair"), "dp"),
        P(("expert", "dp"), None, "pair"),
        P(("expert", "dp"), "pair", None),
    )
    return jax.shard_map(
        per_device,
        mesh=mesh,
        in_specs=placed,
        out_specs=(
            P(("groups", "expert", "pair"), "dp"),
            P(("groups", "dp"), ("expert", "pair"), None, None),
            P(("groups", "dp"), ("expert", "pair"), None, None),
            P(("groups", "expert", "dp"), None, "pair"),
            P(("groups", "expert", "dp"), "pair", None),
        ),
        check_vma=False,
    )
```
